32 devices in a mesh: seq: 8 (over z, x), head: 4 (over y, core).
Axes of the slice: x: 2, y: 2, z: 4, core: 2. Of those that a mesh axis runs over, the one named last changes fastest.
Arguments:
- tokens: bfloat16 [2048, 1024], P('seq'), may hold values from -6 to 6
- attn_gain: bfloat16 [1024], replicated, may hold values from 0.099609375 to 1.8984375
- w_in: bfloat16 [1024, 3072], P(None, 'head'), may hold values from -0.1875 to 0.1875
- conv_weight: bfloat16 [4, 2048], P(None, 'head'), may hold values from -3 to 3
- gate_down: bfloat16 [1024, 16], replicated, may hold values from -0.1875 to 0.1875
- gate_up: bfloat16 [16, 512], P(None, 'head'), may hold values from -1.5 to 1.5
- forget_bias: bfloat16 [512], P('head'), may hold values from 0.5 to 10
- out_gain: bfloat16 [256], replicated, may hold values from 0.099609375 to 1.8984375
- w_out: bfloat16 [1024, 1024], P('head'), may hold values from -0.375 to 0.375
- mlp_gain: bfloat16 [1024], replicated, may hold values from 0.099609375 to 1.8984375
- w_gate_up: bfloat16 [1024, 5632], P(None, 'head'), may hold values from -0.1875 to 0.1875
- w_down: bfloat16 [2816, 1024], P('head'), may hold values from -0.21875 to 0.21875
- cotangent: bfloat16 [2048, 1024], P('seq'), may hold values from -6 to 6
Outputs:
- block_out: bfloat16 [2048, 1024], P('seq')
- grad_tokens: bfloat16 [2048, 1024], P('seq')
- grad_attn_gain: float32 [1024], P('seq')
- grad_w_in: float32 [1024, 3072], P('seq', 'head')
- grad_conv_weight: float32 [4, 2048], P(None, 'head')
- grad_gate_down: float32 [1024, 16], P('seq')
- grad_gate_up: float32 [16, 512], P(None, 'head')
- grad_forget_bias: float32 [512], P('head')
- grad_out_gain: float32 [256], replicated
- grad_w_out: float32 [1024, 1024], P('head', 'seq')
- grad_mlp_gain: float32 [1024], P('seq')
- grad_w_gate_up: float32 [1024, 5632], P('seq', 'head')
- grad_w_down: float32 [2816, 1024], P('head', 'seq')
The draws below stay inside these ranges and needn't reach their ends.
All inputs are finite; a program needn't handle non-finite values.
Results may differ from the reference program's by a relative error of at most 0.02.
The reference program's roundings to bfloat16 on the way count: a program that leaves them out, or rounds other values in their place, can miss the bound.
Values may be sent and summed in bfloat16 or wider, within the bound.
A program may use at most 128 MiB of HBM per device.

```python
import jax
import jax.numpy as jnp
from jax import lax

D = 1024
H = 4
DK = 128
DV = 256
FF = 2816
RANK = 16
CONV = 4
SPAN = 64
LENGTH = 2048


def draw_forget_bias(key, part):
    key = jax.random.fold_in(key, 7)
    return jax.random.uniform(key, (H * DK,), jnp.float32, 0.5, 9.0).astype(jnp.bfloat16)


def block_scale(stream_key, extent, cuts, smallest, top_value):
    def one(position, blocks):
        heights = jax.random.uniform(jax.random.fold_in(jax.random.fold_in(stream_key, 6), position), (blocks,), jnp.float32, smallest / len(cuts), top_value / len(cuts))
        return jnp.repeat(jnp.exp(heights), extent[position] // blocks).reshape((-1,) + (1,) * (len(extent) - position - 1))

    level = one(*cuts[0])
    for cut in cuts[1:]:
        level = level * one(*cut)
    return level


def gaussian(rng, shape, spread, reach, shards=(), held_as=jnp.bfloat16):
    array = jax.random.normal(rng, shape, jnp.float32) * spread
    if len(shards) > 0:
        array = block_scale(rng, shape, shards, -0.22, 0.18) * array
    return jnp.clip(array, min=-reach, max=reach).astype(held_as)


def setup_inputs(seed: int = 0) -> dict:
    keys = jax.random.split(jax.random.key(seed), 14)
    tokens = gaussian(keys[0], (LENGTH, D), 1.0, 6.0, ((0, 8),))
    attn_gain = jnp.clip(1.0 + 0.18 * jax.random.normal(keys[1], (D,), jnp.float32), 0.099609375, 1.8984375).astype(jnp.bfloat16)
    w_in = gaussian(keys[2], (D, H * (2 * DK + 2 * DV)), D ** -0.5, 0.1875, ((1, 4),))
    conv_weight = gaussian(keys[3], (CONV, H * (2 * DK + DV)), CONV ** -0.5, 3.0, ((1, 4),))
    gate_down = gaussian(keys[4], (D, RANK), D ** -0.5, 0.1875)
    gate_up = gaussian(keys[5], (RANK, H * DK), RANK ** -0.5, 1.5, ((1, 4),))
    forget_bias = draw_forget_bias(jax.random.fold_in(keys[13], 71), 0)
    out_gain = jnp.clip(1.0 + 0.18 * jax.random.normal(keys[7], (DV,), jnp.float32), 0.099609375, 1.8984375).astype(jnp.bfloat16)
    w_out = gaussian(keys[8], (H * DV, D), DV ** -0.5, 0.375, ((0, 4),))
    mlp_gain = jnp.clip(1.0 + 0.18 * jax.random.normal(keys[9], (D,), jnp.float32), 0.099609375, 1.8984375).astype(jnp.bfloat16)
    w_gate_up = gaussian(keys[10], (D, 2 * FF), D ** -0.5, 0.1875, ((1, 4),))
    w_down = gaussian(keys[11], (FF, D), (FF // 4) ** -0.5, 0.21875, ((0, 4),))
    cotangent = gaussian(keys[12], (LENGTH, D), 1.0, 6.0, ((0, 8),))
    return {"tokens": tokens, "attn_gain": attn_gain, "w_in": w_in, "conv_weight": conv_weight, "gate_down": gate_down, "gate_up": gate_up, "forget_bias": forget_bias, "out_gain": out_gain, "w_out": w_out, "mlp_gain": mlp_gain, "w_gate_up": w_gate_up, "w_down": w_down, "cotangent": cotangent}


@jax.custom_vjp
def low(v):
    return lax.optimization_barrier(v.astype(jnp.bfloat16)).astype(jnp.float32)

@jax.custom_vjp
def low_back(v):
    return v

def low_keep(v):
    return (low(v), None)

def low_pass(kept, grad):
    return (grad,)

def back_keep(v):
    return (v, None)

def back_low(kept, grad):
    return (low(grad),)
low.defvjp(low_keep, low_pass)
low_back.defvjp(back_keep, back_low)
norm_eps = 1e-05

def product_exact(left, right):
    return jnp.dot(left, right, precision=lax.Precision.HIGHEST)

def rms_norm(values, gain):
    return values * lax.rsqrt(lax.optimization_barrier(jnp.mean(values * values, axis=-1, keepdims=True)) + norm_eps) * gain

def span_step(carried, pieces):
    queries, key_rows, value_rows, log_decay = pieces
    cumulative = jnp.cumsum(log_decay, axis=0)
    positions = jnp.arange(queries.shape[0])
    causal = positions[:, None] >= positions[None, :]
    query_in = queries * jnp.exp(cumulative)
    scores = jnp.where(causal, product_exact(query_in, (key_rows * jnp.exp(-cumulative)).T), 0.0)
    outputs = product_exact(scores, value_rows) + product_exact(query_in, carried)
    ending = cumulative[-1]
    carried = jnp.exp(ending)[:, None] * carried + product_exact((key_rows * jnp.exp(ending - cumulative)).T, value_rows)
    return (carried, outputs)

def gla_head(queries, key_rows, value_rows, log_decay):
    blocks = queries.shape[0] // SPAN
    pieces = (queries.reshape(blocks, SPAN, -1), key_rows.reshape(blocks, SPAN, -1), value_rows.reshape(blocks, SPAN, -1), log_decay.reshape(blocks, SPAN, -1))
    initial = jnp.zeros((queries.shape[1], value_rows.shape[1]), jnp.float32)
    ending, outputs = lax.scan(jax.checkpoint(span_step), initial, pieces)
    return outputs.reshape(queries.shape[0], -1)

def causal_conv(values, kernel):
    padded = jnp.concatenate([jnp.zeros((CONV - 1, values.shape[1]), jnp.float32), values], axis=0)
    total = jnp.zeros_like(values)
    for offset in range(CONV):
        total = total + kernel[offset] * padded[offset:offset + values.shape[0]]
    return total

def forward(tokens, attn_gain, w_in, conv_weight, gate_down, gate_up, forget_bias, out_gain, w_out, mlp_gain, w_gate_up, w_down):
    length = tokens.shape[0]
    normed = low(rms_norm(tokens, attn_gain))
    projected = product_exact(normed, w_in).reshape(length, H, 2 * DK + 2 * DV)
    mixed_pre = low_back(low(projected[:, :, :2 * DK + DV]))
    out_gate = low_back(projected[:, :, 2 * DK + DV:])
    conv_pre = causal_conv(mixed_pre.reshape(length, H * (2 * DK + DV)), conv_weight)
    convolved = low(jax.nn.silu(conv_pre)).reshape(length, H, 2 * DK + DV)
    queries = convolved[:, :, :DK] * DK ** (-0.5)
    key_rows = convolved[:, :, DK:2 * DK]
    value_rows = convolved[:, :, 2 * DK:]
    low_rank = product_exact(normed, gate_down)
    logits = product_exact(low_rank, gate_up) + forget_bias
    log_decay = (jax.nn.log_sigmoid(logits) / 16.0).reshape(length, H, DK)
    attended = jax.vmap(gla_head, in_axes=1, out_axes=1)(queries, key_rows, value_rows, log_decay)
    gated = low(rms_norm(attended, out_gain) * jax.nn.silu(out_gate))
    residual = tokens + low_back(product_exact(gated.reshape(length, H * DV), w_out))
    normed_mlp = low(rms_norm(residual, mlp_gain))
    gate_up_val = low_back(product_exact(normed_mlp, w_gate_up)).reshape(length, H, 2, FF // H)
    hidden = low(jax.nn.silu(gate_up_val[:, :, 0]) * gate_up_val[:, :, 1]).reshape(length, FF)
    return residual + low_back(product_exact(hidden, w_down))

def reference(tokens, attn_gain, w_in, conv_weight, gate_down, gate_up, forget_bias, out_gain, w_out, mlp_gain, w_gate_up, w_down, cotangent):
    inputs = [item.astype(jnp.float32) for item in (tokens, attn_gain, w_in, conv_weight, gate_down, gate_up, forget_bias, out_gain, w_out, mlp_gain, w_gate_up, w_down)]
    output, pullback = jax.vjp(forward, *inputs)
    grads = pullback(cotangent.astype(jnp.float32))
    return (output.astype(jnp.bfloat16), grads[0].astype(jnp.bfloat16), grads[1], grads[2], grads[3], grads[4], grads[5], grads[6], grads[7], grads[8], grads[9], grads[10], grads[11])
```

```python
import functools

import jax
import jax.numpy as jnp
from jax import lax
from jax.experimental import pallas as pl
from jax.experimental.pallas import tpu as pltpu
from jax.sharding import PartitionSpec as P

SPAN = 64


norm_eps = 1e-05

MESH = pl.DeviceIdType.MESH
LIMIT = 24 * 1024 * 1024
low_type = jnp.bfloat16


def from_behind(value, axis, steps):
    count = lax.axis_size(axis)
    leading, last = (max(0, -steps), min(count, count - steps))
    return lax.ppermute(value, axis, [(source, source + steps) for source in range(leading, last)])


def product_exact(left, right):
    return jnp.dot(left, right, precision=lax.Precision.HIGHEST)


def product_plain(left, right):
    return jnp.dot(left, right, preferred_element_type=jnp.float32)


def product_lead(left, right):
    return lax.dot_general(
        left, right, (((0,), (0,)), ((), ())), preferred_element_type=jnp.float32
    )


def product_last(left, right):
    return lax.dot_general(
        left, right, (((1,), (1,)), ((), ())), preferred_element_type=jnp.float32
    )


def rms_norm(values, gain):
    return values * lax.rsqrt(jnp.mean(values * values, axis=-1, keepdims=True) + norm_eps) * gain


def gate_norm(attended, gain, out_gate):
    return rms_norm(attended, gain) * jax.nn.silu(out_gate)


def swiglu(gate_up_val):
    half_width = gate_up_val.shape[1] // 2
    return jax.nn.silu(gate_up_val[:, :half_width]) * gate_up_val[:, half_width:]


def decay_of(logits):
    return jax.nn.log_sigmoid(logits) / 16.0


def greet(axis, peers):
    barrier = pltpu.get_barrier_semaphore()
    for peer in peers:
        pl.semaphore_signal(barrier, inc=1, device_id={axis: peer}, device_id_type=MESH)
    pl.semaphore_wait(barrier, len(peers))


def comm_params(collective):
    return pltpu.CompilerParams(
        collective_id=collective, has_side_effects=True, vmem_limit_bytes=LIMIT
    )


def vmem_specs(count):
    return [pl.BlockSpec(memory_space=pltpu.VMEM)] * count


def head_sum_kernel(pieces, x_ref, o_ref, s1, r1, s2, r2, s3, r3, send, recv):
    me = lax.axis_index("head")
    near = me + 1 - 2 * lax.rem(me, 2)
    far = lax.rem(me + 2, 4)
    half = x_ref.shape[0] // 2
    step = half // pieces
    mine = lax.rem(me, 2) * half
    other = half - mine
    greet("head", (near, far))

    def copy(stage, piece, source, target, peer):
        return pltpu.make_async_remote_copy(
            src_ref=source.at[pl.ds(piece * step, step)],
            dst_ref=target.at[pl.ds(piece * step, step)],
            send_sem=send.at[stage, piece],
            recv_sem=recv.at[stage, piece],
            device_id={"head": peer},
            device_id_type=MESH,
        )

    def rows(base, piece):
        return pl.ds(pl.multiple_of(base + piece * step, 16), step)

    copies = []
    for piece in range(pieces):
        local = pl.ds(piece * step, step)
        s1[local, :] = x_ref[rows(other, piece), :].astype(low_type)
        copies.append(copy(0, piece, s1, r1, near))
        copies[-1].start()
    second = []
    for piece in range(pieces):
        local = pl.ds(piece * step, step)
        copies[piece].wait()
        s2[local, :] = (x_ref[rows(mine, piece), :] + r1[local, :].astype(jnp.float32)).astype(
            low_type
        )
        second.append(copy(1, piece, s2, r2, far))
        second[-1].start()
    third = []
    for piece in range(pieces):
        local = pl.ds(piece * step, step)
        second[piece].wait()
        total = s2[local, :].astype(jnp.float32) + r2[local, :].astype(jnp.float32)
        s3[local, :] = total
        third.append(copy(2, piece, s3, r3, near))
        third[-1].start()
        o_ref[rows(mine, piece), :] = total
    for piece in range(pieces):
        local = pl.ds(piece * step, step)
        third[piece].wait()
        o_ref[rows(other, piece), :] = r3[local, :]


def head_sum(value, collective, pieces=4):
    rows, width = value.shape
    half = (rows // 2, width)
    return pl.pallas_call(
        functools.partial(head_sum_kernel, pieces),
        out_shape=jax.ShapeDtypeStruct(value.shape, jnp.float32),
        in_specs=vmem_specs(1),
        out_specs=vmem_specs(1)[0],
        scratch_shapes=[
            pltpu.VMEM(half, low_type),
            pltpu.VMEM(half, low_type),
            pltpu.VMEM(half, low_type),
            pltpu.VMEM(half, low_type),
            pltpu.VMEM(half, jnp.float32),
            pltpu.VMEM(half, jnp.float32),
            pltpu.SemaphoreType.DMA((3, pieces)),
            pltpu.SemaphoreType.DMA((3, pieces)),
        ],
        compiler_params=comm_params(collective),
        cost_estimate=pl.CostEstimate(flops=0, bytes_accessed=40_000_000, transcendentals=0),
    )(value)


def seq_peers(count):
    me = lax.axis_index("seq")
    return [lax.rem(me + distance, count) for distance in range(1, count)]


def seq_copies(count, source_of, gathered, send, recv):
    me = lax.axis_index("seq")
    return [
        pltpu.make_async_remote_copy(
            src_ref=source_of(peer),
            dst_ref=gathered.at[me],
            send_sem=send.at[place],
            recv_sem=recv.at[place],
            device_id={"seq": peer},
            device_id_type=MESH,
        )
        for place, peer in enumerate(seq_peers(count))
    ]


def seq_sum_kernel(count, x_ref, o_ref, gathered, send, recv):
    me = lax.axis_index("seq")
    greet("seq", seq_peers(count))
    copies = seq_copies(count, lambda peer: x_ref.at[peer], gathered, send, recv)
    for one in copies:
        one.start()
    gathered[me] = x_ref[me]
    for one in copies:
        one.wait()
    total = gathered[0]
    for place in range(1, count):
        total = total + gathered[place]
    o_ref[...] = total


def seq_sum(value, collective):
    count, rows, width = value.shape
    return pl.pallas_call(
        functools.partial(seq_sum_kernel, count),
        out_shape=jax.ShapeDtypeStruct((rows, width), jnp.float32),
        in_specs=vmem_specs(1),
        out_specs=vmem_specs(1)[0],
        scratch_shapes=[
            pltpu.VMEM((count, rows, width), jnp.float32),
            pltpu.SemaphoreType.DMA((count - 1,)),
            pltpu.SemaphoreType.DMA((count - 1,)),
        ],
        compiler_params=comm_params(collective),
        cost_estimate=pl.CostEstimate(flops=0, bytes_accessed=20_000_000, transcendentals=0),
    )(value)


def dot_exact(left, right, left_dim, right_dim):
    return lax.dot_general(
        left,
        right,
        (((left_dim,), (right_dim,)), ((), ())),
        precision=lax.Precision.HIGHEST,
        preferred_element_type=jnp.float32,
    )


def causal_mask(size):
    row = lax.broadcasted_iota(jnp.int32, (size, size), 0)
    column = lax.broadcasted_iota(jnp.int32, (size, size), 1)
    return row >= column


def put_state(gathered, me, state, decay):
    height, width = state.shape
    high = decay.astype(low_type).astype(jnp.float32)
    rest = decay - high
    middle = rest.astype(low_type).astype(jnp.float32)
    last = rest - middle
    place = lax.broadcasted_iota(jnp.int32, (16, width), 0)
    extra = jnp.where(place == 0, high, jnp.where(place == 1, middle, jnp.where(place == 2, last, 0.0)))
    gathered[me, 0:height, :] = state.astype(low_type)
    gathered[me, height : height + 16, :] = extra.astype(low_type)


def join_state(total, gathered, place, taken):
    height = total.shape[0]
    extra = gathered[place, height : height + 16, :].astype(jnp.float32)
    decay = extra[0:1] + extra[1:2] + extra[2:3]
    longer = jnp.exp(decay) * total + gathered[place, 0:height, :].astype(jnp.float32)
    return jnp.where(taken, longer, total)


def mixer_forward_kernel(
    count, conv_ref, decay_ref, attended_ref, total_ref, state_ref, intra, query_in, gathered, send, recv
):
    me = lax.axis_index("seq")
    tok_count, key_width = decay_ref.shape
    spans = tok_count // SPAN
    value_width = attended_ref.shape[1]
    greet("seq", seq_peers(count))
    causal = causal_mask(SPAN)
    ones = causal.astype(jnp.float32)
    state = jnp.zeros((value_width, key_width), jnp.float32)
    before = jnp.zeros((1, key_width), jnp.float32)
    starts = []
    for span in range(spans):
        rows = pl.ds(span * SPAN, SPAN)
        cumulative = dot_exact(ones, decay_ref[rows, :], 1, 0)
        total_ref[rows, :] = cumulative
        keys = conv_ref[rows, key_width : 2 * key_width].astype(jnp.float32)
        values = conv_ref[rows, 2 * key_width :].astype(jnp.float32)
        ending = cumulative[SPAN - 1 : SPAN]
        state_ref[span] = state
        starts.append(before)
        state = jnp.exp(ending) * state + dot_exact(
            values, keys * jnp.exp(ending - cumulative), 0, 0
        )
        before = before + ending
    put_state(gathered, me, state, before)
    copies = seq_copies(count, lambda peer: gathered.at[me], gathered, send, recv)
    for one in copies:
        one.start()
    for span in range(spans):
        rows = pl.ds(span * SPAN, SPAN)
        cumulative = total_ref[rows, :]
        queries = conv_ref[rows, 0:key_width].astype(jnp.float32) * key_width ** (-0.5)
        keys = conv_ref[rows, key_width : 2 * key_width].astype(jnp.float32)
        values = conv_ref[rows, 2 * key_width :].astype(jnp.float32)
        inner = queries * jnp.exp(cumulative)
        query_in[rows, :] = inner
        scores = jnp.where(causal, dot_exact(inner, keys * jnp.exp(-cumulative), 1, 1), 0.0)
        intra[rows, :] = dot_exact(scores, values, 1, 0)
    for one in copies:
        one.wait()
    entering = jnp.zeros((value_width, key_width), jnp.float32)
    for place in range(count - 1):
        entering = join_state(entering, gathered, place, place < me)
    for span in range(spans):
        rows = pl.ds(span * SPAN, SPAN)
        start = state_ref[span] + jnp.exp(starts[span]) * entering
        state_ref[span] = start
        attended_ref[rows, :] = intra[rows, :] + dot_exact(query_in[rows, :], start, 1, 1)


def mixer_forward(convolved, log_decay, value_width, collective):
    count = lax.axis_size("seq")
    tok_count, key_width = log_decay.shape
    spans = tok_count // SPAN
    return pl.pallas_call(
        functools.partial(mixer_forward_kernel, count),
        out_shape=(
            jax.ShapeDtypeStruct((tok_count, value_width), jnp.float32),
            jax.ShapeDtypeStruct((tok_count, key_width), jnp.float32),
            jax.ShapeDtypeStruct((spans, value_width, key_width), jnp.float32),
        ),
        in_specs=vmem_specs(2),
        out_specs=tuple(vmem_specs(3)),
        scratch_shapes=[
            pltpu.VMEM((tok_count, value_width), jnp.float32),
            pltpu.VMEM((tok_count, key_width), jnp.float32),
            pltpu.VMEM((count, value_width + 16, key_width), low_type),
            pltpu.SemaphoreType.DMA((count - 1,)),
            pltpu.SemaphoreType.DMA((count - 1,)),
        ],
        compiler_params=comm_params(collective),
        cost_estimate=pl.CostEstimate(flops=0, bytes_accessed=60_000_000, transcendentals=0),
    )(convolved, log_decay)


def mixer_backward_kernel(
    count,
    conv_ref,
    total_ref,
    state_ref,
    grad_ref,
    conv_grad_ref,
    decay_grad_ref,
    local,
    gathered,
    send,
    recv,
):
    me = lax.axis_index("seq")
    tok_count, key_width = total_ref.shape
    spans = tok_count // SPAN
    value_width = grad_ref.shape[1]
    scale = key_width ** (-0.5)
    greet("seq", seq_peers(count))
    causal = causal_mask(SPAN)
    ones = causal.astype(jnp.float32)
    state = jnp.zeros((value_width, key_width), jnp.float32)
    after = jnp.zeros((1, key_width), jnp.float32)
    ends = [None] * spans
    for span in reversed(range(spans)):
        rows = pl.ds(span * SPAN, SPAN)
        cumulative = total_ref[rows, :]
        ending = cumulative[SPAN - 1 : SPAN]
        inner = conv_ref[rows, 0:key_width].astype(jnp.float32) * scale * jnp.exp(cumulative)
        local[span] = state
        ends[span] = after
        state = jnp.exp(ending) * state + dot_exact(grad_ref[rows, :], inner, 0, 0)
        after = after + ending
    put_state(gathered, me, state, after)
    copies = seq_copies(count, lambda peer: gathered.at[me], gathered, send, recv)
    for one in copies:
        one.start()
    for span in range(spans):
        rows = pl.ds(span * SPAN, SPAN)
        cumulative = total_ref[rows, :]
        inner = conv_ref[rows, 0:key_width].astype(jnp.float32) * scale * jnp.exp(cumulative)
        key_in = conv_ref[rows, key_width : 2 * key_width].astype(jnp.float32) * jnp.exp(
            -cumulative
        )
        values = conv_ref[rows, 2 * key_width :].astype(jnp.float32)
        grad = grad_ref[rows, :]
        scores = jnp.where(causal, dot_exact(inner, key_in, 1, 1), 0.0)
        grad_scores = jnp.where(causal, dot_exact(grad, values, 1, 1), 0.0)
        grad_inner = dot_exact(grad_scores, key_in, 1, 0) + dot_exact(grad, state_ref[span], 1, 0)
        grad_key_in = dot_exact(grad_scores, inner, 0, 0)
        conv_grad_ref[rows, 0:key_width] = grad_inner * (scale * jnp.exp(cumulative))
        conv_grad_ref[rows, key_width : 2 * key_width] = grad_key_in * jnp.exp(-cumulative)
        conv_grad_ref[rows, 2 * key_width :] = dot_exact(scores, grad, 0, 0)
        decay_grad_ref[rows, :] = grad_inner * inner - grad_key_in * key_in
    for one in copies:
        one.wait()
    leaving = jnp.zeros((value_width, key_width), jnp.float32)
    for turn in range(count - 1):
        place = count - 1 - turn
        leaving = join_state(leaving, gathered, place, place > me)
    for span in range(spans):
        rows = pl.ds(span * SPAN, SPAN)
        cumulative = total_ref[rows, :]
        ending = cumulative[SPAN - 1 : SPAN]
        to_end = jnp.exp(ending - cumulative)
        key_end = conv_ref[rows, key_width : 2 * key_width].astype(jnp.float32) * to_end
        values = conv_ref[rows, 2 * key_width :].astype(jnp.float32)
        out_grad = local[span] + jnp.exp(ends[span]) * leaving
        grad_key_end = dot_exact(values, out_grad, 1, 0)
        conv_grad_ref[rows, key_width : 2 * key_width] += grad_key_end * to_end
        conv_grad_ref[rows, 2 * key_width :] += dot_exact(key_end, out_grad, 1, 1)
        through = grad_key_end * key_end
        end_grad = jnp.sum(through, axis=0, keepdims=True) + jnp.exp(ending) * jnp.sum(
            state_ref[span] * out_grad, axis=0, keepdims=True
        )
        decay_grad_ref[rows, :] = (
            dot_exact(ones, decay_grad_ref[rows, :] - through, 0, 0) + end_grad
        )


def mixer_backward(convolved, cumulative, states, grad_attended, collective):
    count = lax.axis_size("seq")
    tok_count, key_width = cumulative.shape
    spans, value_width = states.shape[:2]
    return pl.pallas_call(
        functools.partial(mixer_backward_kernel, count),
        out_shape=(
            jax.ShapeDtypeStruct(convolved.shape, jnp.float32),
            jax.ShapeDtypeStruct((tok_count, key_width), jnp.float32),
        ),
        in_specs=vmem_specs(4),
        out_specs=tuple(vmem_specs(2)),
        scratch_shapes=[
            pltpu.VMEM((spans, value_width, key_width), jnp.float32),
            pltpu.VMEM((count, value_width + 16, key_width), low_type),
            pltpu.SemaphoreType.DMA((count - 1,)),
            pltpu.SemaphoreType.DMA((count - 1,)),
        ],
        compiler_params=comm_params(collective),
        cost_estimate=pl.CostEstimate(flops=0, bytes_accessed=80_000_000, transcendentals=0),
    )(convolved, cumulative, states, grad_attended)


def halve_rows(value, order):
    count = lax.axis_size("seq")
    me = lax.axis_index("seq")
    bits = count.bit_length() - 1
    height, width = value.shape
    left = list(reversed(range(bits)))
    view = value.reshape((2,) * bits + (height // count, width))
    for bit in order(bits):
        dim = left.index(bit)
        own = (me // (1 << bit)) % 2
        sent = lax.dynamic_index_in_dim(view, 1 - own, dim, False)
        kept = lax.dynamic_index_in_dim(view, own, dim, False)
        got = lax.ppermute(
            sent.astype(low_type), "seq", [(place, place ^ (1 << bit)) for place in range(count)]
        )
        view = kept + got.astype(jnp.float32)
        left.remove(bit)
    return view


def upward(bits):
    return list(range(bits))


def near_last(bits):
    return list(range(1, bits)) + [0]


def on_device(
    tokens,
    attn_gain,
    w_in,
    conv_weight,
    gate_down,
    gate_up,
    forget_bias,
    out_gain,
    w_out,
    mlp_gain,
    w_gate_up,
    w_down,
    cotangent,
):
    tok_count = tokens.shape[0]
    qkv_width = conv_weight.shape[1]
    key_width = gate_up.shape[1]
    value_width = out_gain.shape[0]
    rim_rows = conv_weight.shape[0] - 1
    inputs = tokens.astype(jnp.float32)
    attn_gain32 = attn_gain.astype(jnp.float32)
    normed32, attn_norm_back = jax.vjp(rms_norm, inputs, attn_gain32)
    normed = normed32.astype(jnp.bfloat16)
    projected = product_plain(normed, w_in)
    mixed_pre = projected[:, :qkv_width].astype(jnp.bfloat16)
    out_gate = projected[:, qkv_width:]
    prev_rows = from_behind(mixed_pre[tok_count - rim_rows :], "seq", 1)
    extended = jnp.concatenate([prev_rows, mixed_pre], axis=0).astype(jnp.float32)
    kernel = conv_weight.astype(jnp.float32)
    conv_pre = jnp.zeros((tok_count, qkv_width), jnp.float32)
    for offset in range(rim_rows + 1):
        conv_pre = conv_pre + kernel[offset] * extended[offset : offset + tok_count]
    activated, silu_back = jax.vjp(jax.nn.silu, conv_pre)
    convolved = lax.optimization_barrier(activated.astype(jnp.bfloat16))
    low_rank = product_plain(normed, gate_down)
    gate_up32 = gate_up.astype(jnp.float32)
    logits = product_exact(low_rank, gate_up32) + forget_bias.astype(jnp.float32)
    log_decay, decay_back = jax.vjp(decay_of, logits)
    attended, cumulative, states = mixer_forward(convolved, log_decay, value_width, 1)
    out_gain32 = out_gain.astype(jnp.float32)
    gated32, gate_back = jax.vjp(gate_norm, attended, out_gain32, out_gate)
    gated = gated32.astype(jnp.bfloat16)
    mixer_total = head_sum(product_plain(gated, w_out), 2)
    residual = inputs + mixer_total
    mlp_gain32 = mlp_gain.astype(jnp.float32)
    normed_mlp32, mlp_norm_back = jax.vjp(rms_norm, residual, mlp_gain32)
    normed_mlp = normed_mlp32.astype(jnp.bfloat16)
    gate_up_val = product_plain(normed_mlp, w_gate_up)
    hidden32, act_back = jax.vjp(swiglu, gate_up_val)
    hidden = hidden32.astype(jnp.bfloat16)
    mlp_total = lax.psum(product_plain(hidden, w_down).astype(jnp.bfloat16), "head").astype(
        jnp.float32
    )
    block_out = (residual + mlp_total).astype(jnp.bfloat16)
    grad_w_down = halve_rows(product_lead(cotangent, hidden), near_last)
    grad_hidden = product_last(cotangent, w_down)
    grad_gate_up_val = act_back(grad_hidden)[0].astype(jnp.bfloat16)
    grad_w_gate_up = halve_rows(product_lead(normed_mlp, grad_gate_up_val), upward)
    normed_mlp_grad = head_sum(product_last(grad_gate_up_val, w_gate_up), 3)
    grad_resid_part, grad_mlp_gain = mlp_norm_back(normed_mlp_grad)
    grad_residual = cotangent.astype(jnp.float32) + grad_resid_part
    grad_res_low = grad_residual.astype(jnp.bfloat16)
    grad_w_out = halve_rows(product_lead(grad_res_low, gated), near_last)
    grad_gated = product_last(grad_res_low, w_out)
    grad_attended, grad_out_gain, grad_out_gate = gate_back(grad_gated)
    grad_convolved, grad_decay = mixer_backward(convolved, cumulative, states, grad_attended, 4)
    grad_conv_pre = silu_back(grad_convolved)[0]
    grad_extended = jnp.zeros((tok_count + rim_rows, qkv_width), jnp.float32)
    kernel_rows = []
    for offset in range(rim_rows + 1):
        grad_extended = grad_extended + jnp.pad(
            kernel[offset] * grad_conv_pre, ((offset, rim_rows - offset), (0, 0))
        )
        kernel_rows.append(jnp.sum(extended[offset : offset + tok_count] * grad_conv_pre, axis=0))
    grad_kernel = jnp.stack(kernel_rows, axis=0)
    next_rows = from_behind(grad_extended[:rim_rows], "seq", -1)
    grad_pre = grad_extended[rim_rows:] + jnp.pad(next_rows, ((tok_count - rim_rows, 0), (0, 0)))
    grad_projected = jnp.concatenate([grad_pre, grad_out_gate], axis=1).astype(jnp.bfloat16)
    grad_w_in = halve_rows(product_lead(normed, grad_projected), upward)
    normed_grad_part = product_last(grad_projected, w_in)
    grad_logits = decay_back(grad_decay)[0]
    grad_forget_bias = jnp.sum(grad_logits, axis=0)
    grad_gate_up = product_exact(low_rank.T, grad_logits)
    grad_low_rank = product_exact(grad_logits, gate_up32.T)
    rank = gate_down.shape[1]
    width = tokens.shape[1]
    extra = jnp.concatenate(
        [
            grad_low_rank,
            grad_out_gain[:, None],
            jnp.zeros((tok_count, 128 - rank - 1), jnp.float32),
        ],
        axis=1,
    )
    summed = head_sum(jnp.concatenate([normed_grad_part, extra], axis=1), 5)
    summed_normed = summed[:, :width]
    summed_low_rank = summed[:, width : width + rank]
    summed_out_gain = summed[:, width + rank]
    grad_gate_down = lax.dot_general(
        summed_low_rank,
        normed.astype(jnp.float32),
        (((0,), (0,)), ((), ())),
        precision=lax.Precision.HIGHEST,
    )
    total_normed = summed_normed + product_exact(summed_low_rank, gate_down.astype(jnp.float32).T)
    grad_input_part, grad_attn_gain = attn_norm_back(total_normed)
    grad_tokens = (grad_residual + grad_input_part).astype(jnp.bfloat16)
    count = lax.axis_size("seq")
    share = width // count
    for_each = jnp.concatenate(
        [grad_gate_down, grad_attn_gain[None], grad_mlp_gain[None]], axis=0
    ).reshape(rank + 2, count, share)
    for_each = jnp.swapaxes(for_each, 0, 1).reshape(count, -1)
    shared = jnp.concatenate(
        [
            grad_kernel.reshape(-1),
            grad_gate_up.reshape(-1),
            grad_forget_bias,
            summed_out_gain,
        ]
    )
    sizes = (rank * share, share, share)
    length = for_each.shape[1] + shared.shape[0]
    padded = -(-length // 1024) * 1024
    small = jnp.concatenate(
        [
            for_each,
            jnp.broadcast_to(shared, (count, shared.shape[0])),
            jnp.zeros((count, padded - length), jnp.float32),
        ],
        axis=1,
    ).reshape(count, padded // 128, 128)
    sums = seq_sum(small, 6).reshape(-1)
    places = [0]
    for size in sizes + (
        grad_kernel.size,
        grad_gate_up.size,
        grad_forget_bias.size,
        summed_out_gain.size,
    ):
        places.append(places[-1] + size)
    cut = [sums[start:end] for start, end in zip(places[:-1], places[1:])]
    return (
        block_out,
        grad_tokens,
        cut[1],
        grad_w_in,
        cut[3].reshape(grad_kernel.shape),
        cut[0].reshape(rank, share).T,
        cut[4].reshape(grad_gate_up.shape),
        cut[5],
        cut[6],
        grad_w_out.T,
        cut[2],
        grad_w_gate_up,
        grad_w_down.T,
    )


def solution(mesh):
    return jax.shard_map(
        on_device,
        mesh=mesh,
        in_specs=(
            P("seq", None),
            P(),
            P(None, "head"),
            P(None, "head"),
            P(),
            P(None, "head"),
            P("head"),
            P(),
            P("head", None),
            P(),
            P(None, "head"),
            P("head", None),
            P("seq", None),
        ),
        out_specs=(
            P("seq", None),
            P("seq", None),
            P("seq"),
            P("seq", "head"),
            P(None, "head"),
            P("seq", None),
            P(None, "head"),
            P("head"),
            P(),
            P("head", "seq"),
            P("seq"),
            P("seq", "head"),
            P("head", "seq"),
        ),
        check_vma=False,
    )
```

```python
import functools

import jax
import jax.numpy as jnp
from jax import lax
from jax.experimental import pallas as pl
from jax.experimental.pallas import tpu as pltpu
from jax.sharding import PartitionSpec as P

SPAN = 64


norm_eps = 1e-05

MESH = pl.DeviceIdType.MESH
LIMIT = 24 * 1024 * 1024
low_type = jnp.bfloat16


def from_behind(value, axis, steps):
    count = lax.axis_size(axis)
    leading, last = (max(0, -steps), min(count, count - steps))
    return lax.ppermute(value, axis, [(source, source + steps) for source in range(leading, last)])


def product_exact(left, right):
    return jnp.dot(left, right, precision=lax.Precision.HIGHEST)


def product_plain(left, right):
    return jnp.dot(left, right, preferred_element_type=jnp.float32)


def product_lead(left, right):
    return lax.dot_general(
        left, right, (((0,), (0,)), ((), ())), preferred_element_type=jnp.float32
    )


def product_last(left, right):
    return lax.dot_general(
        left, right, (((1,), (1,)), ((), ())), preferred_element_type=jnp.float32
    )


def rms_norm(values, gain):
    return values * lax.rsqrt(jnp.mean(values * values, axis=-1, keepdims=True) + norm_eps) * gain


def gate_norm(attended, gain, out_gate):
    return rms_norm(attended, gain) * jax.nn.silu(out_gate)


def swiglu(gate_up_val):
    half_width = gate_up_val.shape[1] // 2
    return jax.nn.silu(gate_up_val[:, :half_width]) * gate_up_val[:, half_width:]


def decay_of(logits):
    return jax.nn.log_sigmoid(logits) / 16.0


def greet(axis, peers):
    barrier = pltpu.get_barrier_semaphore()
    for peer in peers:
        pl.semaphore_signal(barrier, inc=1, device_id={axis: peer}, device_id_type=MESH)
    pl.semaphore_wait(barrier, len(peers))


def comm_params(collective):
    return pltpu.CompilerParams(
        collective_id=collective, has_side_effects=True, vmem_limit_bytes=LIMIT
    )


def vmem_specs(count):
    return [pl.BlockSpec(memory_space=pltpu.VMEM)] * count


def head_sum_kernel(pieces, x_ref, o_ref, s1, r1, s2, r2, s3, r3, send, recv):
    me = lax.axis_index("head")
    near = me + 1 - 2 * lax.rem(me, 2)
    far = lax.rem(me + 2, 4)
    half = x_ref.shape[0] // 2
    step = half // pieces
    mine = lax.rem(me, 2) * half
    other = half - mine
    greet("head", (near, far))

    def copy(stage, piece, source, target, peer):
        return pltpu.make_async_remote_copy(
            src_ref=source.at[pl.ds(piece * step, step)],
            dst_ref=target.at[pl.ds(piece * step, step)],
            send_sem=send.at[stage, piece],
            recv_sem=recv.at[stage, piece],
            device_id={"head": peer},
            device_id_type=MESH,
        )

    def rows(base, piece):
        return pl.ds(pl.multiple_of(base + piece * step, 16), step)

    copies = []
    for piece in range(pieces):
        local = pl.ds(piece * step, step)
        s1[local, :] = x_ref[rows(other, piece), :].astype(low_type)
        copies.append(copy(0, piece, s1, r1, near))
        copies[-1].start()
    second = []
    for piece in range(pieces):
        local = pl.ds(piece * step, step)
        copies[piece].wait()
        s2[local, :] = (x_ref[rows(mine, piece), :] + r1[local, :].astype(jnp.float32)).astype(
            low_type
        )
        second.append(copy(1, piece, s2, r2, far))
        second[-1].start()
    third = []
    for piece in range(pieces):
        local = pl.ds(piece * step, step)
        second[piece].wait()
        total = s2[local, :].astype(jnp.float32) + r2[local, :].astype(jnp.float32)
        s3[local, :] = total
        third.append(copy(2, piece, s3, r3, near))
        third[-1].start()
        o_ref[rows(mine, piece), :] = total
    for piece in range(pieces):
        local = pl.ds(piece * step, step)
        third[piece].wait()
        o_ref[rows(other, piece), :] = r3[local, :]


def head_sum(value, collective, pieces=4):
    rows, width = value.shape
    half = (rows // 2, width)
    return pl.pallas_call(
        functools.partial(head_sum_kernel, pieces),
        out_shape=jax.ShapeDtypeStruct(value.shape, jnp.float32),
        in_specs=vmem_specs(1),
        out_specs=vmem_specs(1)[0],
        scratch_shapes=[
            pltpu.VMEM(half, low_type),
            pltpu.VMEM(half, low_type),
            pltpu.VMEM(half, low_type),
            pltpu.VMEM(half, low_type),
            pltpu.VMEM(half, jnp.float32),
            pltpu.VMEM(half, jnp.float32),
            pltpu.SemaphoreType.DMA((3, pieces)),
            pltpu.SemaphoreType.DMA((3, pieces)),
        ],
        compiler_params=comm_params(collective),
        cost_estimate=pl.CostEstimate(flops=0, bytes_accessed=2_000_000, transcendentals=0),
    )(value)


def seq_peers(count):
    me = lax.axis_index("seq")
    return [lax.rem(me + distance, count) for distance in range(1, count)]


def seq_copies(count, source_of, gathered, send, recv):
    me = lax.axis_index("seq")
    return [
        pltpu.make_async_remote_copy(
            src_ref=source_of(peer),
            dst_ref=gathered.at[me],
            send_sem=send.at[place],
            recv_sem=recv.at[place],
            device_id={"seq": peer},
            device_id_type=MESH,
        )
        for place, peer in enumerate(seq_peers(count))
    ]


def seq_sum_kernel(count, x_ref, o_ref, gathered, send, recv):
    me = lax.axis_index("seq")
    greet("seq", seq_peers(count))
    copies = seq_copies(count, lambda peer: x_ref.at[peer], gathered, send, recv)
    for one in copies:
        one.start()
    gathered[me] = x_ref[me]
    for one in copies:
        one.wait()
    total = gathered[0]
    for place in range(1, count):
        total = total + gathered[place]
    o_ref[...] = total


def seq_sum(value, collective):
    count, rows, width = value.shape
    return pl.pallas_call(
        functools.partial(seq_sum_kernel, count),
        out_shape=jax.ShapeDtypeStruct((rows, width), jnp.float32),
        in_specs=vmem_specs(1),
        out_specs=vmem_specs(1)[0],
        scratch_shapes=[
            pltpu.VMEM((count, rows, width), jnp.float32),
            pltpu.SemaphoreType.DMA((count - 1,)),
            pltpu.SemaphoreType.DMA((count - 1,)),
        ],
        compiler_params=comm_params(collective),
        cost_estimate=pl.CostEstimate(flops=0, bytes_accessed=2_000_000, transcendentals=0),
    )(value)


def dot_one(left, right, left_dim, right_dim):
    return lax.dot_general(
        left, right, (((left_dim,), (right_dim,)), ((), ())), preferred_element_type=jnp.float32
    )


def terms(value, count):
    parts = []
    for _ in range(count):
        parts.append(value.astype(low_type))
        value = value - parts[-1].astype(jnp.float32)
    return parts


def dot_exact(left, right, left_dim, right_dim, count=2):
    lefts = [left] if left.dtype == low_type else terms(left, count)
    rights = [right] if right.dtype == low_type else terms(right, count)
    total = None
    for rank in reversed(range(count)):
        for one in range(rank + 1):
            if one < len(lefts) and rank - one < len(rights):
                product = dot_one(lefts[one], rights[rank - one], left_dim, right_dim)
                total = product if total is None else total + product
    return total


def causal_mask(size):
    row = lax.broadcasted_iota(jnp.int32, (size, size), 0)
    column = lax.broadcasted_iota(jnp.int32, (size, size), 1)
    return row >= column


def put_state(gathered, me, state, decay):
    height, width = state.shape
    high = decay.astype(low_type).astype(jnp.float32)
    rest = decay - high
    middle = rest.astype(low_type).astype(jnp.float32)
    last = rest - middle
    place = lax.broadcasted_iota(jnp.int32, (16, width), 0)
    extra = jnp.where(place == 0, high, jnp.where(place == 1, middle, jnp.where(place == 2, last, 0.0)))
    gathered[me, 0:height, :] = state.astype(low_type)
    gathered[me, height : height + 16, :] = extra.astype(low_type)


def join_state(total, gathered, place, taken):
    height = total.shape[0]
    extra = gathered[place, height : height + 16, :].astype(jnp.float32)
    decay = extra[0:1] + extra[1:2] + extra[2:3]
    longer = jnp.exp(decay) * total + gathered[place, 0:height, :].astype(jnp.float32)
    return jnp.where(taken, longer, total)


def mixer_forward_kernel(
    count, conv_ref, decay_ref, attended_ref, total_ref, state_ref, intra, query_in, gathered, send, recv
):
    me = lax.axis_index("seq")
    tok_count, key_width = decay_ref.shape
    spans = tok_count // SPAN
    value_width = attended_ref.shape[1]
    greet("seq", seq_peers(count))
    causal = causal_mask(SPAN)
    ones = causal.astype(jnp.float32).astype(low_type)
    state = jnp.zeros((value_width, key_width), jnp.float32)
    before = jnp.zeros((1, key_width), jnp.float32)
    starts = []
    for span in range(spans):
        rows = pl.ds(span * SPAN, SPAN)
        cumulative = dot_exact(ones, decay_ref[rows, :], 1, 0, 3)
        total_ref[rows, :] = cumulative
        keys = conv_ref[rows, key_width : 2 * key_width].astype(jnp.float32)
        values = conv_ref[rows, 2 * key_width :]
        ending = cumulative[SPAN - 1 : SPAN]
        state_ref[span] = state
        starts.append(before)
        state = jnp.exp(ending) * state + dot_exact(
            values, keys * jnp.exp(ending - cumulative), 0, 0
        )
        before = before + ending
    put_state(gathered, me, state, before)
    copies = seq_copies(count, lambda peer: gathered.at[me], gathered, send, recv)
    for one in copies:
        one.start()
    for span in range(spans):
        rows = pl.ds(span * SPAN, SPAN)
        cumulative = total_ref[rows, :]
        queries = conv_ref[rows, 0:key_width].astype(jnp.float32) * key_width ** (-0.5)
        keys = conv_ref[rows, key_width : 2 * key_width].astype(jnp.float32)
        values = conv_ref[rows, 2 * key_width :]
        inner = queries * jnp.exp(cumulative)
        query_in[rows, :] = inner
        scores = jnp.where(causal, dot_exact(inner, keys * jnp.exp(-cumulative), 1, 1), 0.0)
        intra[rows, :] = dot_exact(scores, values, 1, 0)
    for one in copies:
        one.wait()
    entering = jnp.zeros((value_width, key_width), jnp.float32)
    for place in range(count - 1):
        entering = join_state(entering, gathered, place, place < me)
    for span in range(spans):
        rows = pl.ds(span * SPAN, SPAN)
        start = state_ref[span] + jnp.exp(starts[span]) * entering
        state_ref[span] = start
        attended_ref[rows, :] = intra[rows, :] + dot_exact(query_in[rows, :], start, 1, 1)


def mixer_forward(convolved, log_decay, value_width, collective):
    count = lax.axis_size("seq")
    tok_count, key_width = log_decay.shape
    spans = tok_count // SPAN
    return pl.pallas_call(
        functools.partial(mixer_forward_kernel, count),
        out_shape=(
            jax.ShapeDtypeStruct((tok_count, value_width), jnp.float32),
            jax.ShapeDtypeStruct((tok_count, key_width), jnp.float32),
            jax.ShapeDtypeStruct((spans, value_width, key_width), jnp.float32),
        ),
        in_specs=vmem_specs(2),
        out_specs=tuple(vmem_specs(3)),
        scratch_shapes=[
            pltpu.VMEM((tok_count, value_width), jnp.float32),
            pltpu.VMEM((tok_count, key_width), jnp.float32),
            pltpu.VMEM((count, value_width + 16, key_width), low_type),
            pltpu.SemaphoreType.DMA((count - 1,)),
            pltpu.SemaphoreType.DMA((count - 1,)),
        ],
        compiler_params=comm_params(collective),
        cost_estimate=pl.CostEstimate(flops=0, bytes_accessed=2_000_000, transcendentals=0),
    )(convolved, log_decay)


def mixer_backward_kernel(
    count,
    conv_ref,
    total_ref,
    state_ref,
    grad_ref,
    conv_grad_ref,
    decay_grad_ref,
    local,
    gathered,
    send,
    recv,
):
    me = lax.axis_index("seq")
    tok_count, key_width = total_ref.shape
    spans = tok_count // SPAN
    value_width = grad_ref.shape[1]
    scale = key_width ** (-0.5)
    greet("seq", seq_peers(count))
    causal = causal_mask(SPAN)
    ones = causal.astype(jnp.float32).astype(low_type)
    state = jnp.zeros((value_width, key_width), jnp.float32)
    after = jnp.zeros((1, key_width), jnp.float32)
    ends = [None] * spans
    for span in reversed(range(spans)):
        rows = pl.ds(span * SPAN, SPAN)
        cumulative = total_ref[rows, :]
        ending = cumulative[SPAN - 1 : SPAN]
        inner = conv_ref[rows, 0:key_width].astype(jnp.float32) * scale * jnp.exp(cumulative)
        local[span] = state
        ends[span] = after
        state = jnp.exp(ending) * state + dot_exact(grad_ref[rows, :], inner, 0, 0)
        after = after + ending
    put_state(gathered, me, state, after)
    copies = seq_copies(count, lambda peer: gathered.at[me], gathered, send, recv)
    for one in copies:
        one.start()
    for span in range(spans):
        rows = pl.ds(span * SPAN, SPAN)
        cumulative = total_ref[rows, :]
        inner = conv_ref[rows, 0:key_width].astype(jnp.float32) * scale * jnp.exp(cumulative)
        key_in = conv_ref[rows, key_width : 2 * key_width].astype(jnp.float32) * jnp.exp(
            -cumulative
        )
        values = conv_ref[rows, 2 * key_width :]
        grad = grad_ref[rows, :]
        scores = jnp.where(causal, dot_exact(inner, key_in, 1, 1), 0.0)
        grad_scores = jnp.where(causal, dot_exact(grad, values, 1, 1), 0.0)
        grad_inner = dot_exact(grad_scores, key_in, 1, 0) + dot_exact(grad, state_ref[span], 1, 0)
        grad_key_in = dot_exact(grad_scores, inner, 0, 0)
        conv_grad_ref[rows, 0:key_width] = grad_inner * (scale * jnp.exp(cumulative))
        conv_grad_ref[rows, key_width : 2 * key_width] = grad_key_in * jnp.exp(-cumulative)
        conv_grad_ref[rows, 2 * key_width :] = dot_exact(scores, grad, 0, 0)
        decay_grad_ref[rows, :] = grad_inner * inner - grad_key_in * key_in
    for one in copies:
        one.wait()
    leaving = jnp.zeros((value_width, key_width), jnp.float32)
    for turn in range(count - 1):
        place = count - 1 - turn
        leaving = join_state(leaving, gathered, place, place > me)
    for span in range(spans):
        rows = pl.ds(span * SPAN, SPAN)
        cumulative = total_ref[rows, :]
        ending = cumulative[SPAN - 1 : SPAN]
        to_end = jnp.exp(ending - cumulative)
        key_end = conv_ref[rows, key_width : 2 * key_width].astype(jnp.float32) * to_end
        values = conv_ref[rows, 2 * key_width :]
        out_grad = local[span] + jnp.exp(ends[span]) * leaving
        grad_key_end = dot_exact(values, out_grad, 1, 0)
        conv_grad_ref[rows, key_width : 2 * key_width] += grad_key_end * to_end
        conv_grad_ref[rows, 2 * key_width :] += dot_exact(key_end, out_grad, 1, 1)
        through = grad_key_end * key_end
        end_grad = jnp.sum(through, axis=0, keepdims=True) + jnp.exp(ending) * jnp.sum(
            state_ref[span] * out_grad, axis=0, keepdims=True
        )
        decay_grad_ref[rows, :] = (
            dot_exact(ones, decay_grad_ref[rows, :] - through, 0, 0, 3) + end_grad
        )


def mixer_backward(convolved, cumulative, states, grad_attended, collective):
    count = lax.axis_size("seq")
    tok_count, key_width = cumulative.shape
    spans, value_width = states.shape[:2]
    return pl.pallas_call(
        functools.partial(mixer_backward_kernel, count),
        out_shape=(
            jax.ShapeDtypeStruct(convolved.shape, jnp.float32),
            jax.ShapeDtypeStruct((tok_count, key_width), jnp.float32),
        ),
        in_specs=vmem_specs(4),
        out_specs=tuple(vmem_specs(2)),
        scratch_shapes=[
            pltpu.VMEM((spans, value_width, key_width), jnp.float32),
            pltpu.VMEM((count, value_width + 16, key_width), low_type),
            pltpu.SemaphoreType.DMA((count - 1,)),
            pltpu.SemaphoreType.DMA((count - 1,)),
        ],
        compiler_params=comm_params(collective),
        cost_estimate=pl.CostEstimate(flops=0, bytes_accessed=2_000_000, transcendentals=0),
    )(convolved, cumulative, states, grad_attended)


def exchange(sent, bit):
    count = lax.axis_size("seq")
    return lax.ppermute(sent, "seq", [(place, place ^ (1 << bit)) for place in range(count)])


def bit_of_me(bit):
    return (lax.axis_index("seq") // (1 << bit)) % 2


def lay_columns_kernel(places, share, x_ref, o_ref):
    for turn, place in enumerate(places):
        o_ref[:, turn * share : (turn + 1) * share] = x_ref[:, place * share : (place + 1) * share]


def lay_columns(value, places, share):
    if share % 128:
        return jnp.concatenate([value[:, p * share : (p + 1) * share] for p in places], axis=1)
    return pl.pallas_call(
        functools.partial(lay_columns_kernel, places, share),
        out_shape=jax.ShapeDtypeStruct(value.shape, value.dtype),
        in_specs=vmem_specs(1),
        out_specs=vmem_specs(1)[0],
        compiler_params=pltpu.CompilerParams(vmem_limit_bytes=LIMIT),
        cost_estimate=pl.CostEstimate(flops=0, bytes_accessed=1_000_000, transcendentals=0),
    )(value)


def begin(left, right, order):
    count = lax.axis_size("seq")
    share = left.shape[1] // count
    places = sorted(range(count), key=lambda place: [(place >> bit) % 2 for bit in order])
    laid = lay_columns(left, places, share)
    half = left.shape[1] // 2
    own = bit_of_me(order[0])
    sent_left = lax.dynamic_slice_in_dim(laid, (1 - own) * half, half, 1)
    kept_left = lax.dynamic_slice_in_dim(laid, own * half, half, 1)
    return (product_lead(sent_left, right).astype(low_type), product_lead(kept_left, right))


def split_half(total, bit):
    half = total.shape[0] // 2
    own = bit_of_me(bit)
    return (
        lax.dynamic_slice_in_dim(total, (1 - own) * half, half, 0).astype(low_type),
        lax.dynamic_slice_in_dim(total, own * half, half, 0),
    )


def finish(sent, kept, order):
    total = kept + exchange(sent, order[0]).astype(jnp.float32)
    for bit in order[1:]:
        sent, kept = split_half(total, bit)
        total = kept + exchange(sent, bit).astype(jnp.float32)
    return total


def advance(got, kept, bit):
    return split_half(kept + got.astype(jnp.float32), bit)


together = lax.optimization_barrier


def on_device(
    tokens,
    attn_gain,
    w_in,
    conv_weight,
    gate_down,
    gate_up,
    forget_bias,
    out_gain,
    w_out,
    mlp_gain,
    w_gate_up,
    w_down,
    cotangent,
):
    tok_count = tokens.shape[0]
    bits = list(range(lax.axis_size("seq").bit_length() - 1))
    near_first = bits
    near_last = bits[1:] + bits[:1]
    qkv_width = conv_weight.shape[1]
    key_width = gate_up.shape[1]
    value_width = out_gain.shape[0]
    rim_rows = conv_weight.shape[0] - 1
    inputs = tokens.astype(jnp.float32)
    attn_gain32 = attn_gain.astype(jnp.float32)
    normed32, attn_norm_back = jax.vjp(rms_norm, inputs, attn_gain32)
    normed = normed32.astype(jnp.bfloat16)
    projected = product_plain(normed, w_in)
    mixed_pre = projected[:, :qkv_width].astype(jnp.bfloat16)
    out_gate = projected[:, qkv_width:]
    prev_rows = from_behind(mixed_pre[tok_count - rim_rows :], "seq", 1)
    extended = jnp.concatenate([prev_rows, mixed_pre], axis=0).astype(jnp.float32)
    kernel = conv_weight.astype(jnp.float32)
    conv_pre = jnp.zeros((tok_count, qkv_width), jnp.float32)
    for offset in range(rim_rows + 1):
        conv_pre = conv_pre + kernel[offset] * extended[offset : offset + tok_count]
    activated, silu_back = jax.vjp(jax.nn.silu, conv_pre)
    convolved = lax.optimization_barrier(activated.astype(jnp.bfloat16))
    low_rank = product_plain(normed, gate_down)
    gate_up32 = gate_up.astype(jnp.float32)
    logits = product_exact(low_rank, gate_up32) + forget_bias.astype(jnp.float32)
    log_decay, decay_back = jax.vjp(decay_of, logits)
    attended, cumulative, states = mixer_forward(convolved, log_decay, value_width, 1)
    out_gain32 = out_gain.astype(jnp.float32)
    gated32, gate_back = jax.vjp(gate_norm, attended, out_gain32, out_gate)
    gated = gated32.astype(jnp.bfloat16)
    mixer_total = head_sum(product_plain(gated, w_out), 2)
    residual = inputs + mixer_total
    mlp_gain32 = mlp_gain.astype(jnp.float32)
    normed_mlp32, mlp_norm_back = jax.vjp(rms_norm, residual, mlp_gain32)
    normed_mlp = normed_mlp32.astype(jnp.bfloat16)
    gate_up_val = product_plain(normed_mlp, w_gate_up)
    hidden32, act_back = jax.vjp(swiglu, gate_up_val)
    hidden = hidden32.astype(jnp.bfloat16)
    mlp_total = lax.psum(product_plain(hidden, w_down).astype(jnp.bfloat16), "head").astype(
        jnp.float32
    )
    block_out = (residual + mlp_total).astype(jnp.bfloat16)
    down_sent, down_kept = begin(cotangent, hidden, near_last)
    grad_hidden = product_last(cotangent, w_down)
    grad_gate_up_val = act_back(grad_hidden)[0].astype(jnp.bfloat16)
    up_sent, up_kept = begin(normed_mlp, grad_gate_up_val, near_first)
    normed_mlp_part, down_sent, up_sent = together(
        (product_last(grad_gate_up_val, w_gate_up), down_sent, up_sent)
    )
    down_got = exchange(down_sent, near_last[0])
    up_got = exchange(up_sent, near_first[0])
    normed_mlp_grad = head_sum(normed_mlp_part, 3)
    grad_resid_part, grad_mlp_gain = mlp_norm_back(normed_mlp_grad)
    grad_residual = cotangent.astype(jnp.float32) + grad_resid_part
    grad_res_low = grad_residual.astype(jnp.bfloat16)
    out_sent, out_kept = begin(grad_res_low, gated, near_last)
    grad_gated = product_last(grad_res_low, w_out)
    grad_attended, grad_out_gain, grad_out_gate = gate_back(grad_gated)
    grad_attended, out_sent = together((grad_attended, out_sent))
    out_got = exchange(out_sent, near_last[0])
    grad_convolved, grad_decay = mixer_backward(convolved, cumulative, states, grad_attended, 4)
    grad_convolved, grad_decay, down_got, up_got, out_got = together(
        (grad_convolved, grad_decay, down_got, up_got, out_got)
    )
    down_sent, down_kept = advance(down_got, down_kept, near_last[1])
    up_sent, up_kept = advance(up_got, up_kept, near_first[1])
    out_sent, out_kept = advance(out_got, out_kept, near_last[1])
    grad_conv_pre = silu_back(grad_convolved)[0]
    grad_extended = jnp.zeros((tok_count + rim_rows, qkv_width), jnp.float32)
    kernel_rows = []
    for offset in range(rim_rows + 1):
        grad_extended = grad_extended + jnp.pad(
            kernel[offset] * grad_conv_pre, ((offset, rim_rows - offset), (0, 0))
        )
        kernel_rows.append(jnp.sum(extended[offset : offset + tok_count] * grad_conv_pre, axis=0))
    grad_kernel = jnp.stack(kernel_rows, axis=0)
    next_rows = from_behind(grad_extended[:rim_rows], "seq", -1)
    grad_pre = grad_extended[rim_rows:] + jnp.pad(next_rows, ((tok_count - rim_rows, 0), (0, 0)))
    grad_projected = jnp.concatenate([grad_pre, grad_out_gate], axis=1).astype(jnp.bfloat16)
    in_sent, in_kept = begin(normed, grad_projected, near_first)
    normed_grad_part = product_last(grad_projected, w_in)
    grad_logits = decay_back(grad_decay)[0]
    grad_forget_bias = jnp.sum(grad_logits, axis=0)
    grad_gate_up = product_exact(low_rank.T, grad_logits)
    grad_low_rank = product_exact(grad_logits, gate_up32.T)
    rank = gate_down.shape[1]
    width = tokens.shape[1]
    extra = jnp.concatenate(
        [
            grad_low_rank,
            grad_out_gain[:, None],
            jnp.zeros((tok_count, 128 - rank - 1), jnp.float32),
        ],
        axis=1,
    )
    extended_part = jnp.concatenate([normed_grad_part, extra], axis=1)
    extended_part, down_sent, up_sent, out_sent, in_sent = together(
        (extended_part, down_sent, up_sent, out_sent, in_sent)
    )
    down_got = exchange(down_sent, near_last[1])
    up_got = exchange(up_sent, near_first[1])
    out_got = exchange(out_sent, near_last[1])
    in_got = exchange(in_sent, near_first[0])
    summed = head_sum(extended_part, 5)
    summed, down_got, up_got, out_got, in_got = together(
        (summed, down_got, up_got, out_got, in_got)
    )
    down_sent, down_kept = advance(down_got, down_kept, near_last[2])
    up_sent, up_kept = advance(up_got, up_kept, near_first[2])
    out_sent, out_kept = advance(out_got, out_kept, near_last[2])
    in_sent, in_kept = advance(in_got, in_kept, near_first[1])
    summed_normed = summed[:, :width]
    summed_low_rank = summed[:, width : width + rank]
    summed_out_gain = summed[:, width + rank]
    grad_gate_down = lax.dot_general(
        summed_low_rank,
        normed.astype(jnp.float32),
        (((0,), (0,)), ((), ())),
        precision=lax.Precision.HIGHEST,
    )
    total_normed = summed_normed + product_exact(summed_low_rank, gate_down.astype(jnp.float32).T)
    grad_input_part, grad_attn_gain = attn_norm_back(total_normed)
    grad_tokens = (grad_residual + grad_input_part).astype(jnp.bfloat16)
    count = lax.axis_size("seq")
    share = width // count
    for_each = jnp.concatenate(
        [grad_gate_down, grad_attn_gain[None], grad_mlp_gain[None]], axis=0
    ).reshape(rank + 2, count, share)
    for_each = jnp.swapaxes(for_each, 0, 1).reshape(count, -1)
    shared = jnp.concatenate(
        [
            grad_kernel.reshape(-1),
            grad_gate_up.reshape(-1),
            grad_forget_bias,
            summed_out_gain,
        ]
    )
    sizes = (rank * share, share, share)
    length = for_each.shape[1] + shared.shape[0]
    padded = -(-length // 1024) * 1024
    small = jnp.concatenate(
        [
            for_each,
            jnp.broadcast_to(shared, (count, shared.shape[0])),
            jnp.zeros((count, padded - length), jnp.float32),
        ],
        axis=1,
    ).reshape(count, padded // 128, 128)
    small, down_sent, up_sent, out_sent, in_sent = together(
        (small, down_sent, up_sent, out_sent, in_sent)
    )
    grad_w_down = finish(down_sent, down_kept, near_last[2:])
    grad_w_gate_up = finish(up_sent, up_kept, near_first[2:])
    grad_w_out = finish(out_sent, out_kept, near_last[2:])
    in_got = exchange(in_sent, near_first[1])
    sums = seq_sum(small, 6)
    sums, in_got = together((sums, in_got))
    grad_w_in = finish(*advance(in_got, in_kept, near_first[2]), near_first[2:])
    sums = sums.reshape(-1)
    places = [0]
    for size in sizes + (
        grad_kernel.size,
        grad_gate_up.size,
        grad_forget_bias.size,
        summed_out_gain.size,
    ):
        places.append(places[-1] + size)
    cut = [sums[start:end] for start, end in zip(places[:-1], places[1:])]
    return (
        block_out,
        grad_tokens,
        cut[1],
        grad_w_in,
        cut[3].reshape(grad_kernel.shape),
        cut[0].reshape(rank, share).T,
        cut[4].reshape(grad_gate_up.shape),
        cut[5],
        cut[6],
        grad_w_out.T,
        cut[2],
        grad_w_gate_up,
        grad_w_down.T,
    )


def solution(mesh):
    return jax.shard_map(
        on_device,
        mesh=mesh,
        in_specs=(
            P("seq", None),
            P(),
            P(None, "head"),
            P(None, "head"),
            P(),
            P(None, "head"),
            P("head"),
            P(),
            P("head", None),
            P(),
            P(None, "head"),
            P("head", None),
            P("seq", None),
        ),
        out_specs=(
            P("seq", None),
            P("seq", None),
            P("seq"),
            P("seq", "head"),
            P(None, "head"),
            P("seq", None),
            P(None, "head"),
            P("head"),
            P(),
            P("head", "seq"),
            P("seq"),
            P("seq", "head"),
            P("head", "seq"),
        ),
        check_vma=False,
    )
```

```python
import functools

import jax
import jax.numpy as jnp
from jax import lax
from jax.experimental import pallas as pl
from jax.experimental.pallas import tpu as pltpu
from jax.sharding import PartitionSpec as P

SPAN = 64


norm_eps = 1e-05

MESH = pl.DeviceIdType.MESH
LIMIT = 24 * 1024 * 1024
low_type = jnp.bfloat16


def from_behind(value, axis, steps):
    count = lax.axis_size(axis)
    leading, last = (max(0, -steps), min(count, count - steps))
    return lax.ppermute(value, axis, [(source, source + steps) for source in range(leading, last)])


def product_exact(left, right):
    return jnp.dot(left, right, precision=lax.Precision.HIGHEST)


def product_plain(left, right):
    return jnp.dot(left, right, preferred_element_type=jnp.float32)


def product_lead(left, right):
    return lax.dot_general(
        left, right, (((0,), (0,)), ((), ())), preferred_element_type=jnp.float32
    )


def product_last(left, right):
    return lax.dot_general(
        left, right, (((1,), (1,)), ((), ())), preferred_element_type=jnp.float32
    )


def rms_norm(values, gain):
    return values * lax.rsqrt(jnp.mean(values * values, axis=-1, keepdims=True) + norm_eps) * gain


def gate_norm(attended, gain, out_gate):
    return rms_norm(attended, gain) * jax.nn.silu(out_gate)


def swiglu(gate_up_val):
    half_width = gate_up_val.shape[1] // 2
    return jax.nn.silu(gate_up_val[:, :half_width]) * gate_up_val[:, half_width:]


def decay_of(logits):
    return jax.nn.log_sigmoid(logits) / 16.0


def greet(axis, peers):
    barrier = pltpu.get_barrier_semaphore()
    for peer in peers:
        pl.semaphore_signal(barrier, inc=1, device_id={axis: peer}, device_id_type=MESH)
    pl.semaphore_wait(barrier, len(peers))


def comm_params(collective):
    return pltpu.CompilerParams(
        collective_id=collective, has_side_effects=True, vmem_limit_bytes=LIMIT
    )


def vmem_specs(count):
    return [pl.BlockSpec(memory_space=pltpu.VMEM)] * count


def head_sum_kernel(pieces, x_ref, o_ref, s1, r1, s2, r2, s3, r3, send, recv):
    me = lax.axis_index("head")
    near = me + 1 - 2 * lax.rem(me, 2)
    far = lax.rem(me + 2, 4)
    half = x_ref.shape[0] // 2
    step = half // pieces
    mine = lax.rem(me, 2) * half
    other = half - mine
    greet("head", (near, far))

    def copy(stage, piece, source, target, peer):
        return pltpu.make_async_remote_copy(
            src_ref=source.at[pl.ds(piece * step, step)],
            dst_ref=target.at[pl.ds(piece * step, step)],
            send_sem=send.at[stage, piece],
            recv_sem=recv.at[stage, piece],
            device_id={"head": peer},
            device_id_type=MESH,
        )

    def rows(base, piece):
        return pl.ds(pl.multiple_of(base + piece * step, 16), step)

    copies = []
    for piece in range(pieces):
        local = pl.ds(piece * step, step)
        s1[local, :] = x_ref[rows(other, piece), :].astype(low_type)
        copies.append(copy(0, piece, s1, r1, near))
        copies[-1].start()
    second = []
    for piece in range(pieces):
        local = pl.ds(piece * step, step)
        copies[piece].wait()
        s2[local, :] = (x_ref[rows(mine, piece), :] + r1[local, :].astype(jnp.float32)).astype(
            low_type
        )
        second.append(copy(1, piece, s2, r2, far))
        second[-1].start()
    third = []
    for piece in range(pieces):
        local = pl.ds(piece * step, step)
        second[piece].wait()
        total = s2[local, :].astype(jnp.float32) + r2[local, :].astype(jnp.float32)
        s3[local, :] = total
        third.append(copy(2, piece, s3, r3, near))
        third[-1].start()
        o_ref[rows(mine, piece), :] = total
    for piece in range(pieces):
        local = pl.ds(piece * step, step)
        third[piece].wait()
        o_ref[rows(other, piece), :] = r3[local, :]


def head_sum(value, collective, pieces=4):
    rows, width = value.shape
    half = (rows // 2, width)
    return pl.pallas_call(
        functools.partial(head_sum_kernel, pieces),
        out_shape=jax.ShapeDtypeStruct(value.shape, jnp.float32),
        in_specs=vmem_specs(1),
        out_specs=vmem_specs(1)[0],
        scratch_shapes=[
            pltpu.VMEM(half, low_type),
            pltpu.VMEM(half, low_type),
            pltpu.VMEM(half, low_type),
            pltpu.VMEM(half, low_type),
            pltpu.VMEM(half, jnp.float32),
            pltpu.VMEM(half, jnp.float32),
            pltpu.SemaphoreType.DMA((3, pieces)),
            pltpu.SemaphoreType.DMA((3, pieces)),
        ],
        compiler_params=comm_params(collective),
        cost_estimate=pl.CostEstimate(flops=0, bytes_accessed=2_000_000, transcendentals=0),
    )(value)


def seq_peers(count):
    me = lax.axis_index("seq")
    return [lax.rem(me + distance, count) for distance in range(1, count)]


def seq_copies(count, source_of, gathered, send, recv):
    me = lax.axis_index("seq")
    return [
        pltpu.make_async_remote_copy(
            src_ref=source_of(peer),
            dst_ref=gathered.at[me],
            send_sem=send.at[place],
            recv_sem=recv.at[place],
            device_id={"seq": peer},
            device_id_type=MESH,
        )
        for place, peer in enumerate(seq_peers(count))
    ]


def seq_sum_kernel(count, x_ref, o_ref, gathered, send, recv):
    me = lax.axis_index("seq")
    greet("seq", seq_peers(count))
    copies = seq_copies(count, lambda peer: x_ref.at[peer], gathered, send, recv)
    for one in copies:
        one.start()
    gathered[me] = x_ref[me]
    for one in copies:
        one.wait()
    total = gathered[0]
    for place in range(1, count):
        total = total + gathered[place]
    o_ref[...] = total


def seq_sum(value, collective):
    count, rows, width = value.shape
    return pl.pallas_call(
        functools.partial(seq_sum_kernel, count),
        out_shape=jax.ShapeDtypeStruct((rows, width), jnp.float32),
        in_specs=vmem_specs(1),
        out_specs=vmem_specs(1)[0],
        scratch_shapes=[
            pltpu.VMEM((count, rows, width), jnp.float32),
            pltpu.SemaphoreType.DMA((count - 1,)),
            pltpu.SemaphoreType.DMA((count - 1,)),
        ],
        compiler_params=comm_params(collective),
        cost_estimate=pl.CostEstimate(flops=0, bytes_accessed=2_000_000, transcendentals=0),
    )(value)


def dot_one(left, right, left_dim, right_dim):
    return lax.dot_general(
        left, right, (((left_dim,), (right_dim,)), ((), ())), preferred_element_type=jnp.float32
    )


def terms(value, count):
    parts = []
    for _ in range(count):
        parts.append(value.astype(low_type))
        value = value - parts[-1].astype(jnp.float32)
    return parts


def dot_exact(left, right, left_dim, right_dim, count=2):
    lefts = [left] if left.dtype == low_type else terms(left, count)
    rights = [right] if right.dtype == low_type else terms(right, count)
    total = None
    for rank in reversed(range(count)):
        for one in range(rank + 1):
            if one < len(lefts) and rank - one < len(rights):
                product = dot_one(lefts[one], rights[rank - one], left_dim, right_dim)
                total = product if total is None else total + product
    return total


def causal_mask(size):
    row = lax.broadcasted_iota(jnp.int32, (size, size), 0)
    column = lax.broadcasted_iota(jnp.int32, (size, size), 1)
    return row >= column


def put_state(gathered, me, state, decay):
    height, width = state.shape
    high = decay.astype(low_type).astype(jnp.float32)
    rest = decay - high
    middle = rest.astype(low_type).astype(jnp.float32)
    last = rest - middle
    place = lax.broadcasted_iota(jnp.int32, (16, width), 0)
    extra = jnp.where(place == 0, high, jnp.where(place == 1, middle, jnp.where(place == 2, last, 0.0)))
    gathered[me, 0:height, :] = state.astype(low_type)
    gathered[me, height : height + 16, :] = extra.astype(low_type)


def join_state(total, gathered, place, taken):
    height = total.shape[0]
    extra = gathered[place, height : height + 16, :].astype(jnp.float32)
    decay = extra[0:1] + extra[1:2] + extra[2:3]
    longer = jnp.exp(decay) * total + gathered[place, 0:height, :].astype(jnp.float32)
    return jnp.where(taken, longer, total)


def mixer_forward_kernel(
    count, conv_ref, decay_ref, attended_ref, total_ref, state_ref, intra, query_in, gathered, send, recv
):
    me = lax.axis_index("seq")
    tok_count, key_width = decay_ref.shape
    spans = tok_count // SPAN
    value_width = attended_ref.shape[1]
    greet("seq", seq_peers(count))
    causal = causal_mask(SPAN)
    ones = causal.astype(jnp.float32).astype(low_type)
    state = jnp.zeros((value_width, key_width), jnp.float32)
    before = jnp.zeros((1, key_width), jnp.float32)
    starts = []
    for span in range(spans):
        rows = pl.ds(span * SPAN, SPAN)
        cumulative = dot_exact(ones, decay_ref[rows, :], 1, 0, 3)
        total_ref[rows, :] = cumulative
        keys = conv_ref[rows, key_width : 2 * key_width].astype(jnp.float32)
        values = conv_ref[rows, 2 * key_width :]
        ending = cumulative[SPAN - 1 : SPAN]
        state_ref[span] = state
        starts.append(before)
        state = jnp.exp(ending) * state + dot_exact(
            values, keys * jnp.exp(ending - cumulative), 0, 0
        )
        before = before + ending
    put_state(gathered, me, state, before)
    copies = seq_copies(count, lambda peer: gathered.at[me], gathered, send, recv)
    for one in copies:
        one.start()
    for span in range(spans):
        rows = pl.ds(span * SPAN, SPAN)
        cumulative = total_ref[rows, :]
        queries = conv_ref[rows, 0:key_width].astype(jnp.float32) * key_width ** (-0.5)
        keys = conv_ref[rows, key_width : 2 * key_width].astype(jnp.float32)
        values = conv_ref[rows, 2 * key_width :]
        inner = queries * jnp.exp(cumulative)
        query_in[rows, :] = inner
        scores = jnp.where(causal, dot_exact(inner, keys * jnp.exp(-cumulative), 1, 1), 0.0)
        intra[rows, :] = dot_exact(scores, values, 1, 0)
    for one in copies:
        one.wait()
    entering = jnp.zeros((value_width, key_width), jnp.float32)
    for place in range(count - 1):
        entering = join_state(entering, gathered, place, place < me)
    for span in range(spans):
        rows = pl.ds(span * SPAN, SPAN)
        start = state_ref[span] + jnp.exp(starts[span]) * entering
        state_ref[span] = start
        attended_ref[rows, :] = intra[rows, :] + dot_exact(query_in[rows, :], start, 1, 1)


def mixer_forward(convolved, log_decay, value_width, collective):
    count = lax.axis_size("seq")
    tok_count, key_width = log_decay.shape
    spans = tok_count // SPAN
    return pl.pallas_call(
        functools.partial(mixer_forward_kernel, count),
        out_shape=(
            jax.ShapeDtypeStruct((tok_count, value_width), jnp.float32),
            jax.ShapeDtypeStruct((tok_count, key_width), jnp.float32),
            jax.ShapeDtypeStruct((spans, value_width, key_width), jnp.float32),
        ),
        in_specs=vmem_specs(2),
        out_specs=tuple(vmem_specs(3)),
        scratch_shapes=[
            pltpu.VMEM((tok_count, value_width), jnp.float32),
            pltpu.VMEM((tok_count, key_width), jnp.float32),
            pltpu.VMEM((count, value_width + 16, key_width), low_type),
            pltpu.SemaphoreType.DMA((count - 1,)),
            pltpu.SemaphoreType.DMA((count - 1,)),
        ],
        compiler_params=comm_params(collective),
        cost_estimate=pl.CostEstimate(flops=0, bytes_accessed=2_000_000, transcendentals=0),
    )(convolved, log_decay)


def mixer_backward_kernel(
    count,
    conv_ref,
    total_ref,
    state_ref,
    grad_ref,
    conv_grad_ref,
    decay_grad_ref,
    local,
    gathered,
    send,
    recv,
):
    me = lax.axis_index("seq")
    tok_count, key_width = total_ref.shape
    spans = tok_count // SPAN
    value_width = grad_ref.shape[1]
    scale = key_width ** (-0.5)
    greet("seq", seq_peers(count))
    causal = causal_mask(SPAN)
    ones = causal.astype(jnp.float32).astype(low_type)
    state = jnp.zeros((value_width, key_width), jnp.float32)
    after = jnp.zeros((1, key_width), jnp.float32)
    ends = [None] * spans
    for span in reversed(range(spans)):
        rows = pl.ds(span * SPAN, SPAN)
        cumulative = total_ref[rows, :]
        ending = cumulative[SPAN - 1 : SPAN]
        inner = conv_ref[rows, 0:key_width].astype(jnp.float32) * scale * jnp.exp(cumulative)
        local[span] = state
        ends[span] = after
        state = jnp.exp(ending) * state + dot_exact(grad_ref[rows, :], inner, 0, 0)
        after = after + ending
    put_state(gathered, me, state, after)
    copies = seq_copies(count, lambda peer: gathered.at[me], gathered, send, recv)
    for one in copies:
        one.start()
    for span in range(spans):
        rows = pl.ds(span * SPAN, SPAN)
        cumulative = total_ref[rows, :]
        inner = conv_ref[rows, 0:key_width].astype(jnp.float32) * scale * jnp.exp(cumulative)
        key_in = conv_ref[rows, key_width : 2 * key_width].astype(jnp.float32) * jnp.exp(
            -cumulative
        )
        values = conv_ref[rows, 2 * key_width :]
        grad = grad_ref[rows, :]
        scores = jnp.where(causal, dot_exact(inner, key_in, 1, 1), 0.0)
        grad_scores = jnp.where(causal, dot_exact(grad, values, 1, 1), 0.0)
        grad_inner = dot_exact(grad_scores, key_in, 1, 0) + dot_exact(grad, state_ref[span], 1, 0)
        grad_key_in = dot_exact(grad_scores, inner, 0, 0)
        conv_grad_ref[rows, 0:key_width] = grad_inner * (scale * jnp.exp(cumulative))
        conv_grad_ref[rows, key_width : 2 * key_width] = grad_key_in * jnp.exp(-cumulative)
        conv_grad_ref[rows, 2 * key_width :] = dot_exact(scores, grad, 0, 0)
        decay_grad_ref[rows, :] = grad_inner * inner - grad_key_in * key_in
    for one in copies:
        one.wait()
    leaving = jnp.zeros((value_width, key_width), jnp.float32)
    for turn in range(count - 1):
        place = count - 1 - turn
        leaving = join_state(leaving, gathered, place, place > me)
    for span in range(spans):
        rows = pl.ds(span * SPAN, SPAN)
        cumulative = total_ref[rows, :]
        ending = cumulative[SPAN - 1 : SPAN]
        to_end = jnp.exp(ending - cumulative)
        key_end = conv_ref[rows, key_width : 2 * key_width].astype(jnp.float32) * to_end
        values = conv_ref[rows, 2 * key_width :]
        out_grad = local[span] + jnp.exp(ends[span]) * leaving
        grad_key_end = dot_exact(values, out_grad, 1, 0)
        conv_grad_ref[rows, key_width : 2 * key_width] += grad_key_end * to_end
        conv_grad_ref[rows, 2 * key_width :] += dot_exact(key_end, out_grad, 1, 1)
        through = grad_key_end * key_end
        end_grad = jnp.sum(through, axis=0, keepdims=True) + jnp.exp(ending) * jnp.sum(
            state_ref[span] * out_grad, axis=0, keepdims=True
        )
        decay_grad_ref[rows, :] = (
            dot_exact(ones, decay_grad_ref[rows, :] - through, 0, 0, 3) + end_grad
        )


def mixer_backward(convolved, cumulative, states, grad_attended, collective):
    count = lax.axis_size("seq")
    tok_count, key_width = cumulative.shape
    spans, value_width = states.shape[:2]
    return pl.pallas_call(
        functools.partial(mixer_backward_kernel, count),
        out_shape=(
            jax.ShapeDtypeStruct(convolved.shape, jnp.float32),
            jax.ShapeDtypeStruct((tok_count, key_width), jnp.float32),
        ),
        in_specs=vmem_specs(4),
        out_specs=tuple(vmem_specs(2)),
        scratch_shapes=[
            pltpu.VMEM((spans, value_width, key_width), jnp.float32),
            pltpu.VMEM((count, value_width + 16, key_width), low_type),
            pltpu.SemaphoreType.DMA((count - 1,)),
            pltpu.SemaphoreType.DMA((count - 1,)),
        ],
        compiler_params=comm_params(collective),
        cost_estimate=pl.CostEstimate(flops=0, bytes_accessed=2_000_000, transcendentals=0),
    )(convolved, cumulative, states, grad_attended)


def exchange(sent, bit):
    count = lax.axis_size("seq")
    return lax.ppermute(sent, "seq", [(place, place ^ (1 << bit)) for place in range(count)])


def bit_of_me(bit):
    return (lax.axis_index("seq") // (1 << bit)) % 2


def lay_columns_kernel(places, share, x_ref, o_ref):
    for turn, place in enumerate(places):
        o_ref[:, turn * share : (turn + 1) * share] = x_ref[:, place * share : (place + 1) * share]


def lay_columns(value, places, share):
    if share % 128:
        return jnp.concatenate([value[:, p * share : (p + 1) * share] for p in places], axis=1)
    return pl.pallas_call(
        functools.partial(lay_columns_kernel, places, share),
        out_shape=jax.ShapeDtypeStruct(value.shape, value.dtype),
        in_specs=vmem_specs(1),
        out_specs=vmem_specs(1)[0],
        compiler_params=pltpu.CompilerParams(vmem_limit_bytes=LIMIT),
        cost_estimate=pl.CostEstimate(flops=0, bytes_accessed=1_000_000, transcendentals=0),
    )(value)


def begin(left, right, order):
    count = lax.axis_size("seq")
    share = left.shape[1] // count
    places = sorted(range(count), key=lambda place: [(place >> bit) % 2 for bit in order])
    laid = lay_columns(left, places, share)
    half = left.shape[1] // 2
    own = bit_of_me(order[0])
    sent_left = lax.dynamic_slice_in_dim(laid, (1 - own) * half, half, 1)
    kept_left = lax.dynamic_slice_in_dim(laid, own * half, half, 1)
    return (product_lead(sent_left, right).astype(low_type), product_lead(kept_left, right))


def split_half(total, bit):
    half = total.shape[0] // 2
    own = bit_of_me(bit)
    return (
        lax.dynamic_slice_in_dim(total, (1 - own) * half, half, 0).astype(low_type),
        lax.dynamic_slice_in_dim(total, own * half, half, 0),
    )


def finish(sent, kept, order):
    total = kept + exchange(sent, order[0]).astype(jnp.float32)
    for bit in order[1:]:
        sent, kept = split_half(total, bit)
        total = kept + exchange(sent, bit).astype(jnp.float32)
    return total


def advance(got, kept, bit):
    return split_half(kept + got.astype(jnp.float32), bit)


together = lax.optimization_barrier


def on_device(
    tokens,
    attn_gain,
    w_in,
    conv_weight,
    gate_down,
    gate_up,
    forget_bias,
    out_gain,
    w_out,
    mlp_gain,
    w_gate_up,
    w_down,
    cotangent,
):
    tok_count = tokens.shape[0]
    bits = list(range(lax.axis_size("seq").bit_length() - 1))
    near_first = bits
    near_last = bits[1:] + bits[:1]
    qkv_width = conv_weight.shape[1]
    key_width = gate_up.shape[1]
    value_width = out_gain.shape[0]
    rim_rows = conv_weight.shape[0] - 1
    inputs = tokens.astype(jnp.float32)
    attn_gain32 = attn_gain.astype(jnp.float32)
    normed32, attn_norm_back = jax.vjp(rms_norm, inputs, attn_gain32)
    normed = normed32.astype(jnp.bfloat16)
    projected = product_plain(normed, w_in)
    mixed_pre = projected[:, :qkv_width].astype(jnp.bfloat16)
    out_gate = projected[:, qkv_width:]
    prev_rows = from_behind(mixed_pre[tok_count - rim_rows :], "seq", 1)
    extended = jnp.concatenate([prev_rows, mixed_pre], axis=0).astype(jnp.float32)
    kernel = conv_weight.astype(jnp.float32)
    conv_pre = jnp.zeros((tok_count, qkv_width), jnp.float32)
    for offset in range(rim_rows + 1):
        conv_pre = conv_pre + kernel[offset] * extended[offset : offset + tok_count]
    activated, silu_back = jax.vjp(jax.nn.silu, conv_pre)
    convolved = lax.optimization_barrier(activated.astype(jnp.bfloat16))
    low_rank = product_plain(normed, gate_down)
    gate_up32 = gate_up.astype(jnp.float32)
    logits = product_exact(low_rank, gate_up32) + forget_bias.astype(jnp.float32)
    log_decay, decay_back = jax.vjp(decay_of, logits)
    attended, cumulative, states = mixer_forward(convolved, log_decay, value_width, 1)
    out_gain32 = out_gain.astype(jnp.float32)
    gated32, gate_back = jax.vjp(gate_norm, attended, out_gain32, out_gate)
    gated = gated32.astype(jnp.bfloat16)
    mixer_total = head_sum(product_plain(gated, w_out), 2)
    residual = inputs + mixer_total
    mlp_gain32 = mlp_gain.astype(jnp.float32)
    normed_mlp32, mlp_norm_back = jax.vjp(rms_norm, residual, mlp_gain32)
    normed_mlp = normed_mlp32.astype(jnp.bfloat16)
    gate_up_val = product_plain(normed_mlp, w_gate_up)
    hidden32, act_back = jax.vjp(swiglu, gate_up_val)
    hidden = hidden32.astype(jnp.bfloat16)
    mlp_total = lax.psum(product_plain(hidden, w_down).astype(jnp.bfloat16), "head").astype(
        jnp.float32
    )
    block_out = (residual + mlp_total).astype(jnp.bfloat16)
    down_sent, down_kept = begin(cotangent, hidden, near_last)
    grad_hidden = product_last(cotangent, w_down)
    grad_gate_up_val = act_back(grad_hidden)[0].astype(jnp.bfloat16)
    up_sent, up_kept = begin(normed_mlp, grad_gate_up_val, near_first)
    normed_mlp_part, down_sent = together((product_last(grad_gate_up_val, w_gate_up), down_sent))
    down_got = exchange(down_sent, near_last[0])
    normed_mlp_grad, down_got = together((head_sum(normed_mlp_part, 3), down_got))
    down_sent, down_kept = advance(down_got, down_kept, near_last[1])
    grad_resid_part, grad_mlp_gain = mlp_norm_back(normed_mlp_grad)
    grad_residual = cotangent.astype(jnp.float32) + grad_resid_part
    grad_res_low = grad_residual.astype(jnp.bfloat16)
    out_sent, out_kept = begin(grad_res_low, gated, near_last)
    grad_gated = product_last(grad_res_low, w_out)
    grad_attended, grad_out_gain, grad_out_gate = gate_back(grad_gated)
    grad_convolved, grad_decay = mixer_backward(convolved, cumulative, states, grad_attended, 4)
    grad_convolved, grad_decay, down_sent, up_sent, out_sent = together(
        (grad_convolved, grad_decay, down_sent, up_sent, out_sent)
    )
    up_got = exchange(up_sent, near_first[0])
    down_got = exchange(down_sent, near_last[1])
    out_got = exchange(out_sent, near_last[0])
    grad_conv_pre = silu_back(grad_convolved)[0]
    grad_extended = jnp.zeros((tok_count + rim_rows, qkv_width), jnp.float32)
    kernel_rows = []
    for offset in range(rim_rows + 1):
        grad_extended = grad_extended + jnp.pad(
            kernel[offset] * grad_conv_pre, ((offset, rim_rows - offset), (0, 0))
        )
        kernel_rows.append(jnp.sum(extended[offset : offset + tok_count] * grad_conv_pre, axis=0))
    grad_kernel = jnp.stack(kernel_rows, axis=0)
    next_rows = from_behind(grad_extended[:rim_rows], "seq", -1)
    grad_pre = grad_extended[rim_rows:] + jnp.pad(next_rows, ((tok_count - rim_rows, 0), (0, 0)))
    grad_projected = jnp.concatenate([grad_pre, grad_out_gate], axis=1).astype(jnp.bfloat16)
    in_sent, in_kept = begin(normed, grad_projected, near_last)
    normed_grad_part = product_last(grad_projected, w_in)
    grad_logits = decay_back(grad_decay)[0]
    grad_forget_bias = jnp.sum(grad_logits, axis=0)
    grad_gate_up = product_exact(low_rank.T, grad_logits)
    grad_low_rank = product_exact(grad_logits, gate_up32.T)
    rank = gate_down.shape[1]
    width = tokens.shape[1]
    extra = jnp.concatenate(
        [
            grad_low_rank,
            grad_out_gain[:, None],
            jnp.zeros((tok_count, 128 - rank - 1), jnp.float32),
        ],
        axis=1,
    )
    extended_part = jnp.concatenate([normed_grad_part, extra], axis=1)
    extended_part, down_got, up_got, out_got = together(
        (extended_part, down_got, up_got, out_got)
    )
    up_sent, up_kept = advance(up_got, up_kept, near_first[1])
    down_sent, down_kept = advance(down_got, down_kept, near_last[2])
    out_sent, out_kept = advance(out_got, out_kept, near_last[1])
    extended_part, down_sent, up_sent, out_sent, in_sent = together(
        (extended_part, down_sent, up_sent, out_sent, in_sent)
    )
    in_got = exchange(in_sent, near_last[0])
    up_got = exchange(up_sent, near_first[1])
    out_got = exchange(out_sent, near_last[1])
    summed = head_sum(extended_part, 5)
    summed, up_got, out_got, in_got = together((summed, up_got, out_got, in_got))
    up_sent, up_kept = advance(up_got, up_kept, near_first[2])
    out_sent, out_kept = advance(out_got, out_kept, near_last[2])
    in_sent, in_kept = advance(in_got, in_kept, near_last[1])
    summed_normed = summed[:, :width]
    summed_low_rank = summed[:, width : width + rank]
    summed_out_gain = summed[:, width + rank]
    grad_gate_down = lax.dot_general(
        summed_low_rank,
        normed.astype(jnp.float32),
        (((0,), (0,)), ((), ())),
        precision=lax.Precision.HIGHEST,
    )
    total_normed = summed_normed + product_exact(summed_low_rank, gate_down.astype(jnp.float32).T)
    grad_input_part, grad_attn_gain = attn_norm_back(total_normed)
    grad_tokens = (grad_residual + grad_input_part).astype(jnp.bfloat16)
    count = lax.axis_size("seq")
    share = width // count
    for_each = jnp.concatenate(
        [grad_gate_down, grad_attn_gain[None], grad_mlp_gain[None]], axis=0
    ).reshape(rank + 2, count, share)
    for_each = jnp.swapaxes(for_each, 0, 1).reshape(count, -1)
    shared = jnp.concatenate(
        [
            grad_kernel.reshape(-1),
            grad_gate_up.reshape(-1),
            grad_forget_bias,
            summed_out_gain,
        ]
    )
    sizes = (rank * share, share, share)
    length = for_each.shape[1] + shared.shape[0]
    padded = -(-length // 1024) * 1024
    small = jnp.concatenate(
        [
            for_each,
            jnp.broadcast_to(shared, (count, shared.shape[0])),
            jnp.zeros((count, padded - length), jnp.float32),
        ],
        axis=1,
    ).reshape(count, padded // 128, 128)
    small, down_sent, up_sent, out_sent, in_sent = together(
        (small, down_sent, up_sent, out_sent, in_sent)
    )
    grad_w_down = finish(down_sent, down_kept, near_last[2:])
    grad_w_gate_up = finish(up_sent, up_kept, near_first[2:])
    grad_w_out = finish(out_sent, out_kept, near_last[2:])
    in_got = exchange(in_sent, near_last[1])
    sums = seq_sum(small, 6)
    sums, in_got = together((sums, in_got))
    grad_w_in = finish(*advance(in_got, in_kept, near_last[2]), near_last[2:])
    sums = sums.reshape(-1)
    places = [0]
    for size in sizes + (
        grad_kernel.size,
        grad_gate_up.size,
        grad_forget_bias.size,
        summed_out_gain.size,
    ):
        places.append(places[-1] + size)
    cut = [sums[start:end] for start, end in zip(places[:-1], places[1:])]
    return (
        block_out,
        grad_tokens,
        cut[1],
        grad_w_in,
        cut[3].reshape(grad_kernel.shape),
        cut[0].reshape(rank, share).T,
        cut[4].reshape(grad_gate_up.shape),
        cut[5],
        cut[6],
        grad_w_out.T,
        cut[2],
        grad_w_gate_up,
        grad_w_down.T,
    )


def solution(mesh):
    return jax.shard_map(
        on_device,
        mesh=mesh,
        in_specs=(
            P("seq", None),
            P(),
            P(None, "head"),
            P(None, "head"),
            P(),
            P(None, "head"),
            P("head"),
            P(),
            P("head", None),
            P(),
            P(None, "head"),
            P("head", None),
            P("seq", None),
        ),
        out_specs=(
            P("seq", None),
            P("seq", None),
            P("seq"),
            P("seq", "head"),
            P(None, "head"),
            P("seq", None),
            P(None, "head"),
            P("head"),
            P(),
            P("head", "seq"),
            P("seq"),
            P("seq", "head"),
            P("head", "seq"),
        ),
        check_vma=False,
    )
```
